32 devices in a mesh: row: 8 (over y, x, core), col: 4 (over z).
Axes of the slice: x: 2, y: 2, z: 4, core: 2. Of those that a mesh axis runs over, the one named last changes fastest.
Arguments:
- retarded: bfloat16 [64, 64, 64, 128], P('row', 'col'), may hold values from -4 to 4
- mirrored: bfloat16 [64, 64, 64, 128], P('col', 'row'), may hold values from -4 to 4
- lesser_panel: bfloat16 [64, 64, 16, 128], P(('col', 'row')), may hold values from -6 to 6
- initial: float32 [64, 16, 128], P(None, 'col'), may hold values from -6 to 6
- retention: float32 [64, 64], P('row'), may hold values from 0.4 to 1, as said below
- phase_angle: float32 [64], replicated, may hold values from -3.140625 to 3.140625
Outputs:
- propagated: float32 [64, 64, 16, 128], P('row', None, 'col')
The draws below stay inside these ranges and needn't reach their ends.
Inputs may be any that keep to these rules, and one draw needn't show every extreme that they name: `retention`: each entry is the share of an orbital's amplitude kept over one step.
All inputs are finite; a program needn't handle non-finite values.
Results may differ from the reference program's by a relative error of at most 0.0026.
Values may be sent and summed in bfloat16 or wider, within the bound.
A program may use at most 128 MiB of HBM per device.

```python
import math
import jax
import jax.numpy as jnp
from jax import lax

ORBITAL_COUNT = 64
P_SIZE = 16
WINDOW_STEPS = 64


def draw_retention(key, part):
    child_random_keys = jax.random.split(jax.random.fold_in(key, 11), 5)
    ranking = jax.random.permutation(child_random_keys[0], ORBITAL_COUNT)
    slow_count = ORBITAL_COUNT // 2
    slow_mask = ranking < slow_count
    spread = jax.random.uniform(child_random_keys[1], (ORBITAL_COUNT,), jnp.float32)
    slow_rate = jnp.exp(jnp.log(0.05 / WINDOW_STEPS) + spread * (jnp.log(0.7 / WINDOW_STEPS) - jnp.log(0.05 / WINDOW_STEPS)))
    fast_rate = jnp.exp(jnp.log(1.0 / 50.0) + spread * (jnp.log(1.0 / 20.0) - jnp.log(1.0 / 50.0)))
    base_rate = jnp.where(slow_mask, slow_rate, fast_rate)
    roughness = jnp.exp(jax.random.uniform(child_random_keys[2], (WINDOW_STEPS, ORBITAL_COUNT), jnp.float32, jnp.log(0.5), jnp.log(2.0)))
    retained_mask = jnp.exp(-base_rate[None, :] * roughness)
    surge_row_list = jax.random.randint(child_random_keys[3], (2,), 0, WINDOW_STEPS)
    time_labels = jnp.arange(WINDOW_STEPS, dtype=jnp.int32)
    surge_event = jnp.any(time_labels[:, None] == surge_row_list[None, :], axis=1)
    surge_decay = jax.random.uniform(child_random_keys[4], (WINDOW_STEPS, ORBITAL_COUNT), jnp.float32, 0.5, 0.8)
    return jnp.where(surge_event[:, None], retained_mask * surge_decay, retained_mask)


def level_of(key, dims, cuts, least, high):
    def one(position, shards_of):
        steps = jax.random.uniform(jax.random.fold_in(jax.random.fold_in(key, 6), position), (shards_of,), jnp.float32, least / len(cuts), high / len(cuts))
        return jnp.repeat(jnp.exp(steps), dims[position] // shards_of).reshape((-1,) + (1,) * (len(dims) - position - 1))

    loudness = one(*cuts[0])
    for cut in cuts[1:]:
        loudness = loudness * one(*cut)
    return loudness


def centred(stream_key, extent, scale, reach, cuts=(), kind=jnp.bfloat16):
    result = scale * jax.random.normal(stream_key, extent, jnp.float32)
    if cuts:
        result = result * level_of(stream_key, extent, cuts, -0.22, 0.18)
    return jnp.clip(result, -reach, reach).astype(kind)


def setup_inputs(seed: int = 0) -> dict:
    key_of = jax.random.split(jax.random.key(seed), 7)
    retarded = centred(key_of[0], (WINDOW_STEPS, WINDOW_STEPS, ORBITAL_COUNT, 2 * ORBITAL_COUNT), 0.7, 4.0, ((0, 8), (1, 4)))
    mirrored = centred(key_of[1], (WINDOW_STEPS, WINDOW_STEPS, ORBITAL_COUNT, 2 * ORBITAL_COUNT), 0.7, 4.0, ((0, 4), (1, 8)))
    lesser_panel = centred(key_of[2], (WINDOW_STEPS, ORBITAL_COUNT, P_SIZE, 2 * ORBITAL_COUNT), 1.0, 6.0, ((0, 32),))
    initial = centred(key_of[3], (ORBITAL_COUNT, P_SIZE, 2 * ORBITAL_COUNT), 1.0, 6.0, ((1, 4),), jnp.float32)
    retention = draw_retention(jax.random.fold_in(key_of[6], 71), 0)
    phase_angle = jnp.clip(jax.random.uniform(key_of[5], (ORBITAL_COUNT,), jnp.float32, -3.140625, 3.140625), -3.140625, 3.140625)
    return dict(retarded=retarded, mirrored=mirrored, lesser_panel=lesser_panel, initial=initial, retention=retention, phase_angle=phase_angle)


def complex_scale(scale_re, scale_im, current):
    orbit_count = current.shape[-1] // 2
    current_re = current[..., :orbit_count]
    current_im = current[..., orbit_count:]
    factor_re = scale_re[:, None, None]
    factor_im = scale_im[:, None, None]
    return jnp.concatenate([factor_re * current_re - factor_im * current_im, factor_re * current_im + factor_im * current_re], axis=-1)

def self_energy(retarded_tile, mirror_tile):
    orbit_count = retarded_tile.shape[-2]
    ret_re = retarded_tile[..., :orbit_count].astype(jnp.float32)
    ret_im = retarded_tile[..., orbit_count:].astype(jnp.float32)
    mirror_re = jnp.swapaxes(mirror_tile[..., :orbit_count], -1, -2).astype(jnp.float32)
    mirror_im = jnp.swapaxes(mirror_tile[..., orbit_count:], -1, -2).astype(jnp.float32)
    square_re = ret_re * ret_re - ret_im * ret_im
    square_im = 2.0 * ret_re * ret_im
    return jnp.concatenate([square_re * mirror_re - square_im * mirror_im, square_re * mirror_im + square_im * mirror_re], axis=-1)

def reference(retarded, mirrored, lesser_panel, initial, retention, phase_angle):
    panel_matrix = lesser_panel.reshape(WINDOW_STEPS * ORBITAL_COUNT, P_SIZE * 2 * ORBITAL_COUNT)
    norm_factor = 1.0 / (ORBITAL_COUNT * math.sqrt(WINDOW_STEPS))
    positions = jnp.arange(WINDOW_STEPS, dtype=jnp.int32)

    def one_time(time_index):
        row_tiles = retarded[time_index]
        mirror_tiles = mirrored[:, time_index]
        energy = self_energy(row_tiles, mirror_tiles)
        energy = jnp.where((positions <= time_index)[:, None, None], energy, 0.0).astype(jnp.bfloat16)
        energy_re = jnp.transpose(energy[..., :ORBITAL_COUNT], (1, 0, 2)).reshape(ORBITAL_COUNT, WINDOW_STEPS * ORBITAL_COUNT)
        energy_im = jnp.transpose(energy[..., ORBITAL_COUNT:], (1, 0, 2)).reshape(ORBITAL_COUNT, WINDOW_STEPS * ORBITAL_COUNT)
        stacked = jnp.concatenate([energy_re, energy_im], axis=0)
        product = jnp.dot(stacked, panel_matrix, preferred_element_type=jnp.float32).reshape(2, ORBITAL_COUNT, P_SIZE, 2, ORBITAL_COUNT)
        integral_re = product[0, :, :, 0] - product[1, :, :, 1]
        integral_im = product[0, :, :, 1] + product[1, :, :, 0]
        return jnp.concatenate([integral_re, integral_im], axis=-1) * norm_factor
    integrals = lax.map(one_time, jnp.arange(WINDOW_STEPS, dtype=jnp.int32))
    rotate_re = retention * jnp.cos(phase_angle)[None, :]
    rotate_im = retention * jnp.sin(phase_angle)[None, :]

    def advance(current, inputs):
        scale_re, scale_im, integral = inputs
        updated = complex_scale(scale_re, scale_im, current + integral)
        return (updated, updated)
    last_state, states = lax.scan(advance, initial, (rotate_re, rotate_im, integrals))
    return states
```

```python
import functools
import math

import jax
import jax.numpy as jnp
from jax import lax
from jax.experimental import pallas as pl
from jax.experimental.pallas import tpu as pltpu
from jax.sharding import PartitionSpec as P

MESH = pl.DeviceIdType.MESH


def kernel(
    NR, NC, TR, TC, O, PS, norm,
    ret, mir, lp, init, fre, fim, rprod, cpow,
    out,
    E, L, acc, tmp, zl, zr, zs, ends, end_out, rp,
    ls, lf, lr, zsend, zrecv_l, zrecv_r, es, er, rs, rr,
):
    r = lax.axis_index("row")
    c = lax.axis_index("col")
    half = lax.rem(r, 2)
    k = r // 2
    pairs = NR // 2
    partner = r + 1 - 2 * half
    last_time = (k + 1) * 2 * TR - 1
    act = c * TC <= last_time
    act_right = jnp.logical_and(c + 1 < NC, (c + 1) * TC <= last_time)
    has_left = c > 0
    n_up = NC - 1 - c

    bar = pltpu.get_barrier_semaphore()

    def greet(j, carry):
        pl.semaphore_signal(bar, inc=1, device_id=(lax.rem(r + j, NR), c), device_id_type=MESH)
        return carry

    lax.fori_loop(1, NR, greet, 0)

    @pl.when(has_left)
    def _():
        pl.semaphore_signal(bar, inc=1, device_id=(r, c - 1), device_id_type=MESH)

    @pl.when(c < NC - 1)
    def _():
        pl.semaphore_signal(bar, inc=1, device_id=(r, c + 1), device_id_type=MESH)

    for q in range(NC):
        L[q, :, r] = lp[q]

    pl.semaphore_wait(
        bar, NR - 1 + jnp.where(has_left, 1, 0) + jnp.where(c < NC - 1, 1, 0)
    )

    def share(i):
        return jnp.where(i < n_up, NC - 1 - i, jnp.where(i < NC - 1, i - n_up, c))

    def row_act(j):
        return c * TC <= (j + 1) * 2 * TR - 1

    def l_direct(i, j):
        q = share(i)
        return pltpu.make_async_remote_copy(
            src_ref=L.at[q, :, r], dst_ref=L.at[q, :, r],
            send_sem=ls.at[i, j], recv_sem=lr.at[i, r],
            device_id=(2 * j + half, c), device_id_type=MESH,
        )

    def l_forward(i, j):
        q = share(i)
        s = 2 * j + half
        return pltpu.make_async_remote_copy(
            src_ref=L.at[q, :, s], dst_ref=L.at[q, :, s],
            send_sem=lf.at[i, j], recv_sem=lr.at[i, s],
            device_id=(partner, c), device_id_type=MESH,
        )

    def l_arrived(i, s):
        q = share(i)
        return pltpu.make_async_remote_copy(
            src_ref=L.at[q, :, s], dst_ref=L.at[q, :, s],
            send_sem=lf.at[i, 0], recv_sem=lr.at[i, s],
            device_id=(partner, c), device_id_type=MESH,
        )

    def others(fn):
        def body(j, carry):
            @pl.when(jnp.logical_and(j != k, row_act(j)))
            def _():
                fn(j)
            return carry

        lax.fori_loop(0, pairs, body, 0)

    def send_share(i, carry):
        others(lambda j: l_direct(i, j).start())

        @pl.when(act)
        def _():
            l_forward(i, k).start()

        return carry

    lax.fori_loop(0, NC, send_share, 0)

    def r_copy(target):
        return pltpu.make_async_remote_copy(
            src_ref=rprod, dst_ref=rp.at[r],
            send_sem=rs.at[target], recv_sem=rr.at[r],
            device_id=(target, c), device_id_type=MESH,
        )

    def later(fn):
        def body(t, carry):
            fn(t)
            return carry

        lax.fori_loop(r + 1, NR, body, 0)

    later(lambda t: r_copy(t).start())

    lane = lax.broadcasted_iota(jnp.int32, (O, 2 * O), 1)
    low = lane < O
    upper = jnp.where(low, 0, 1)

    @pl.when(act)
    def _():
        def energy(t, carry):
            room = r * TR + t - c * TC
            for s2 in range(TC // 2):
                a0 = ret[t, 2 * s2].astype(jnp.float32)
                a1 = ret[t, 2 * s2 + 1].astype(jnp.float32)
                ar = jnp.where(low, a0, pltpu.roll(a1, O, 1))
                ai = jnp.where(low, pltpu.roll(a0, O, 1), a1)
                m = jnp.concatenate([mir[2 * s2, t], mir[2 * s2 + 1, t]], axis=0)
                mt = m.astype(jnp.float32).T
                mr, mi = mt[:O], mt[O:]
                sr = ar * ar - ai * ai
                si = 2.0 * ar * ai
                keep = upper + 2 * s2 <= room
                e_re = jnp.where(keep, sr * mr - si * mi, 0.0)
                e_im = jnp.where(keep, sr * mi + si * mr, 0.0)
                E[t, 0, :, s2 * 2 * O:(s2 + 1) * 2 * O] = e_re.astype(jnp.bfloat16)
                E[t, 1, :, s2 * 2 * O:(s2 + 1) * 2 * O] = e_im.astype(jnp.bfloat16)
            return carry

        lax.fori_loop(0, TR, energy, 0)

    sign = jnp.where(low, -1.0, 1.0).astype(jnp.float32)

    def z_up(q, p, src):
        return pltpu.make_async_remote_copy(
            src_ref=src.at[q, p], dst_ref=zl.at[q, p],
            send_sem=zsend.at[q, p], recv_sem=zrecv_l.at[q, p],
            device_id=(r, c + 1), device_id_type=MESH,
        )

    def z_down(q, p, src):
        return pltpu.make_async_remote_copy(
            src_ref=src.at[q, p], dst_ref=zr.at[q, p],
            send_sem=zsend.at[q, p], recv_sem=zrecv_r.at[q, p],
            device_id=(r, c - 1), device_id_type=MESH,
        )

    def end_copy(p, target):
        return pltpu.make_async_remote_copy(
            src_ref=end_out.at[p], dst_ref=ends.at[r, p],
            send_sem=es.at[p, target], recv_sem=er.at[p, r],
            device_id=(target, c), device_id_type=MESH,
        )

    def combine(h):
        for t in range(TR):
            a = acc[t, 0, :, h * 2 * O:(h + 1) * 2 * O]
            b = acc[t, 1, :, h * 2 * O:(h + 1) * 2 * O]
            tmp[h, t] = (a + sign * pltpu.roll(b, O, 1)) * norm

    def one_share(i, carry):
        q = share(i)

        @pl.when(act)
        def _():
            def pass_on(j, carry):
                @pl.when(j != k)
                def _():
                    l_arrived(i, 2 * j + half).wait_recv()
                    l_forward(i, j).start()
                return carry

            lax.fori_loop(0, pairs, pass_on, 0)

            def from_partner(j, carry):
                l_arrived(i, 2 * j + 1 - half).wait_recv()
                return carry

            lax.fori_loop(0, pairs, from_partner, 0)

        def one_pair(pp, carry):
            @pl.when(act)
            def _():
                depth = TC * O
                rhs = jnp.concatenate(
                    [L[q, 2 * pp].reshape(depth, 2 * O), L[q, 2 * pp + 1].reshape(depth, 2 * O)],
                    axis=1,
                )
                lhs = E[...].reshape(TR * 2 * O, depth)
                acc[...] = jnp.dot(lhs, rhs, preferred_element_type=jnp.float32).reshape(
                    TR, 2, O, 4 * O
                )

            for h in range(2):
                p = 2 * pp + h

                @pl.when(act)
                def _():
                    combine(h)

                @pl.when(jnp.logical_and(i < n_up, has_left))
                def _():
                    z_up(q, p, zs).wait_recv()

                    @pl.when(act)
                    def _():
                        tmp[h] += zl[q, p].astype(jnp.float32)

                @pl.when(jnp.logical_and(i < n_up, act))
                def _():
                    zs[q, p] = tmp[h].astype(jnp.bfloat16)
                    z_up(q, p, zs).start()

                @pl.when(jnp.logical_and(i < n_up, jnp.logical_not(act)))
                def _():
                    z_up(q, p, zl).start()

                @pl.when(jnp.logical_and(jnp.logical_and(i >= n_up, i < NC - 1), act))
                def _():
                    @pl.when(act_right)
                    def _():
                        z_down(q, p, zs).wait_recv()
                        tmp[h] += zr[q, p].astype(jnp.float32)

                    zs[q, p] = tmp[h].astype(jnp.bfloat16)
                    z_down(q, p, zs).start()

                @pl.when(i == NC - 1)
                def _():
                    @pl.when(jnp.logical_not(act))
                    def _():
                        tmp[h] = jnp.zeros_like(tmp[h])

                    @pl.when(has_left)
                    def _():
                        z_up(q, p, zs).wait_recv()
                        tmp[h] += zl[q, p].astype(jnp.float32)

                    @pl.when(act_right)
                    def _():
                        z_down(q, p, zs).wait_recv()
                        tmp[h] += zr[q, p].astype(jnp.float32)

                    x = jnp.zeros((O, 2 * O), jnp.float32)
                    for t in range(TR):
                        v = tmp[h, t]
                        out[p, t] = v
                        x = x + v
                        x = fre[t] * x + fim[t] * pltpu.roll(x, O, 1)
                    end_out[p] = x
                    later(lambda target: end_copy(p, target).start())

            return carry

        return lax.fori_loop(0, PS // 2, one_pair, carry)

    lax.fori_loop(0, NC, one_share, 0)

    def r_arrive(s, carry):
        pltpu.make_async_remote_copy(
            src_ref=rprod, dst_ref=rp.at[s],
            send_sem=rs.at[0], recv_sem=rr.at[s],
            device_id=(partner, c), device_id_type=MESH,
        ).wait_recv()
        return carry

    lax.fori_loop(0, r, r_arrive, 0)

    def finish(p, carry):
        def enter(s, x):
            pltpu.make_async_remote_copy(
                src_ref=end_out.at[p], dst_ref=ends.at[s, p],
                send_sem=es.at[p, 0], recv_sem=er.at[p, s],
                device_id=(partner, c), device_id_type=MESH,
            ).wait_recv()
            kept = jnp.broadcast_to(rp[s, 0:1, :], (2 * O, 2 * O)).T[:O]
            turned = cpow[0] * x + cpow[1] * pltpu.roll(x, O, 1)
            return kept * turned + ends[s, p]

        x = lax.fori_loop(0, r, enter, init[p])
        for t in range(TR):
            x = x + out[p, t]
            x = fre[t] * x + fim[t] * pltpu.roll(x, O, 1)
            out[p, t] = x
        return carry

    lax.fori_loop(0, PS, finish, 0)

    later(lambda t: r_copy(t).wait_send())

    def drain_share(i, carry):
        q = share(i)
        others(lambda j: l_direct(i, j).wait_send())

        @pl.when(act)
        def _():
            def one(j, carry):
                l_forward(i, j).wait_send()
                return carry

            lax.fori_loop(0, pairs, one, 0)

        def z_one(p, carry):
            @pl.when(i < n_up)
            def _():
                z_up(q, p, zs).wait_send()

            @pl.when(jnp.logical_and(jnp.logical_and(i >= n_up, i < NC - 1), act))
            def _():
                z_down(q, p, zs).wait_send()

            return carry

        lax.fori_loop(0, PS, z_one, 0)
        return carry

    lax.fori_loop(0, NC, drain_share, 0)

    def drain_end(p, carry):
        later(lambda t: end_copy(p, t).wait_send())
        return carry

    lax.fori_loop(0, PS, drain_end, 0)


def per_device(retarded, mirrored, lesser_panel, initial, retention, phase_angle):
    NR = lax.axis_size("row")
    NC = lax.axis_size("col")
    TR, TC, O = retarded.shape[0], retarded.shape[1], retarded.shape[2]
    S2, PN = lesser_panel.shape[0], lesser_panel.shape[2]
    PS = PN // NC
    SK = S2 * O
    norm = 1.0 / (O * math.sqrt(TR * NR))
    lp = jnp.transpose(lesser_panel, (2, 0, 1, 3)).reshape(NC, PS, SK, 2 * O)
    init = jnp.transpose(initial, (1, 0, 2))
    cos, sin = jnp.cos(phase_angle), jnp.sin(phase_angle)
    sign = jnp.concatenate([-jnp.ones((O,), jnp.float32), jnp.ones((O,), jnp.float32)])
    fre = jnp.broadcast_to((retention * cos)[:, :, None], (TR, O, 2 * O))
    fim = (retention * sin)[:, :, None] * sign
    pow_re, pow_im = cos, sin
    kept = retention[0]
    for t in range(1, TR):
        pow_re, pow_im = pow_re * cos - pow_im * sin, pow_re * sin + pow_im * cos
        kept = kept * retention[t]
    cpow = jnp.stack(
        [jnp.broadcast_to(pow_re[:, None], (O, 2 * O)), pow_im[:, None] * sign]
    )
    rprod = jnp.broadcast_to(jnp.concatenate([kept, kept])[None], (8, 2 * O))
    f32, bf16 = jnp.float32, jnp.bfloat16
    dma = pltpu.SemaphoreType.DMA
    states = pl.pallas_call(
        functools.partial(kernel, NR, NC, TR, TC, O, PS, norm),
        out_shape=jax.ShapeDtypeStruct((PS, TR, O, 2 * O), f32),
        in_specs=[pl.BlockSpec(memory_space=pltpu.VMEM)] * 8,
        out_specs=pl.BlockSpec(memory_space=pltpu.VMEM),
        scratch_shapes=[
            pltpu.VMEM((TR, 2, O, TC * O), bf16),
            pltpu.VMEM((NC, PS, NR, SK, 2 * O), bf16),
            pltpu.VMEM((TR, 2, O, 4 * O), f32),
            pltpu.VMEM((2, TR, O, 2 * O), f32),
            pltpu.VMEM((NC, PS, TR, O, 2 * O), bf16),
            pltpu.VMEM((NC, PS, TR, O, 2 * O), bf16),
            pltpu.VMEM((NC, PS, TR, O, 2 * O), bf16),
            pltpu.VMEM((NR, PS, O, 2 * O), f32),
            pltpu.VMEM((PS, O, 2 * O), f32),
            pltpu.VMEM((NR, 8, 2 * O), f32),
            dma((NC, NR // 2)),
            dma((NC, NR // 2)),
            dma((NC, NR)),
            dma((NC, PS)),
            dma((NC, PS)),
            dma((NC, PS)),
            dma((PS, NR)),
            dma((PS, NR)),
            dma((NR,)),
            dma((NR,)),
        ],
        compiler_params=pltpu.CompilerParams(
            collective_id=0, has_side_effects=True, vmem_limit_bytes=56 * 1024 * 1024
        ),
    )(retarded, mirrored, lp, init, fre, fim, rprod, cpow)
    return jnp.transpose(states, (1, 2, 0, 3))


def solution(mesh):
    return jax.shard_map(
        per_device,
        mesh=mesh,
        in_specs=(
            P("row", "col", None, None),
            P("col", "row", None, None),
            P(("col", "row"), None, None, None),
            P(None, "col", None),
            P("row", None),
            P(),
        ),
        out_specs=P("row", None, "col", None),
        check_vma=False,
    )
```

```python
import functools
import math

import jax
import jax.numpy as jnp
from jax import lax
from jax.experimental import pallas as pl
from jax.experimental.pallas import tpu as pltpu
from jax.sharding import PartitionSpec as P

MESH = pl.DeviceIdType.MESH


def kernel(
    NR, NC, TR, TC, O, PS, XS, norm,
    ret_in, mir_in, panel, initial, retention, phase,
    out,
    ret, mir, init, fre, fim, rprod, kre, kim, local_sem,
    E, L, acc, tmp, zl, zr, zs, ends, end_out, pair_end, chip_end, rp,
    l1, l2, lf, lr, zsend, zrecv_l, zrecv_r, es, er, ps, pr, rs, rr,
):
    r = lax.axis_index("row")
    c = lax.axis_index("col")
    half = lax.rem(r, 2)
    k = r // 2
    pairs = NR // 2
    YS = pairs // XS
    partner = r + 1 - 2 * half
    last_time = (k + 1) * 2 * TR - 1
    act = c * TC <= last_time
    act_right = jnp.logical_and(c + 1 < NC, (c + 1) * TC <= last_time)
    has_left = c > 0
    n_up = NC - 1 - c

    ret_load = pltpu.make_async_copy(ret_in, ret, local_sem.at[0])
    mir_load = pltpu.make_async_copy(mir_in, mir, local_sem.at[1])
    ret_load.start()
    mir_load.start()

    bar = pltpu.get_barrier_semaphore()

    def greet(j, carry):
        pl.semaphore_signal(bar, inc=1, device_id=(lax.rem(r + j, NR), c), device_id_type=MESH)
        return carry

    lax.fori_loop(1, NR, greet, 0)

    @pl.when(has_left)
    def _():
        pl.semaphore_signal(bar, inc=1, device_id=(r, c - 1), device_id_type=MESH)

    @pl.when(c < NC - 1)
    def _():
        pl.semaphore_signal(bar, inc=1, device_id=(r, c + 1), device_id_type=MESH)

    for s in range(panel.shape[0]):
        turned = jnp.swapaxes(panel[s].astype(jnp.float32), 0, 1).astype(jnp.bfloat16)
        for q in range(NC):
            L[q, :, r, s * O:(s + 1) * O] = turned[q * PS:(q + 1) * PS]
    kept = retention[0:1]
    for t in range(1, TR):
        kept = kept * retention[t:t + 1]
    rprod[...] = jnp.broadcast_to(jnp.concatenate([kept, kept], axis=1), rprod.shape)

    pl.semaphore_wait(
        bar, NR - 1 + jnp.where(has_left, 1, 0) + jnp.where(c < NC - 1, 1, 0)
    )

    both = jnp.minimum(n_up, c)

    def goes_up(i):
        turn = jnp.where(i < 2 * both, lax.rem(i, 2) == 0, n_up > c)
        return jnp.logical_and(i < NC - 1, turn)

    def share(i):
        nth = jnp.where(i < 2 * both, i // 2, i - both)
        return jnp.where(i < NC - 1, jnp.where(goes_up(i), NC - 1 - nth, nth), c)

    n1 = jnp.where(half == 0, XS, YS)
    n2 = jnp.where(half == 0, YS, XS)
    m1 = jnp.where(half == 0, lax.rem(k, XS), k // XS)
    m2 = jnp.where(half == 0, k // XS, lax.rem(k, XS))

    def chip(a1, a2):
        return jnp.where(half == 0, a2 * XS + a1, a1 * XS + a2)

    def panel_copy(i, source, target, send_sem):
        q = share(i)
        return pltpu.make_async_remote_copy(
            src_ref=L.at[q, :, source], dst_ref=L.at[q, :, source],
            send_sem=send_sem, recv_sem=lr.at[i, source],
            device_id=(target, c), device_id_type=MESH,
        )

    def l_first(i, n):
        return panel_copy(i, r, 2 * chip(n, m2) + half, l1.at[i, n])

    def l_second(i, s1, n):
        return panel_copy(i, 2 * chip(s1, m2) + half, 2 * chip(m1, n) + half, l2.at[i, s1, n])

    def l_forward(i, j):
        return panel_copy(i, 2 * j + half, partner, lf.at[i, j])

    def l_arrived(i, source):
        return panel_copy(i, source, partner, lf.at[i, 0])

    def loop(count, fn, skip=None):
        def body(n, carry):
            if skip is None:
                fn(n)
            else:
                @pl.when(n != skip)
                def _():
                    fn(n)
            return carry

        lax.fori_loop(0, count, body, 0)

    def first_hop(i):
        loop(n1, lambda n: l_first(i, n).start(), m1)

        @pl.when(act)
        def _():
            l_forward(i, k).start()

    def second_hop(i):
        loop(n2, lambda n: l_second(i, m1, n).start(), m2)

        def relay(s1):
            source = chip(s1, m2)
            l_arrived(i, 2 * source + half).wait_recv()
            loop(n2, lambda n: l_second(i, s1, n).start(), m2)

            @pl.when(act)
            def _():
                l_forward(i, source).start()

        loop(n1, relay, m1)

    def last_hop(i):
        def line(s2):
            def one(s1):
                source = chip(s1, s2)
                l_arrived(i, 2 * source + half).wait_recv()

                @pl.when(act)
                def _():
                    l_forward(i, source).start()

            loop(n1, one)

        loop(n2, line, m2)

        @pl.when(act)
        def _():
            loop(pairs, lambda j: l_arrived(i, 2 * j + 1 - half).wait_recv())

    for i in range(min(2, NC)):
        first_hop(i)

    def r_copy(target):
        return pltpu.make_async_remote_copy(
            src_ref=rprod, dst_ref=rp.at[r],
            send_sem=rs.at[target], recv_sem=rr.at[r],
            device_id=(target, c), device_id_type=MESH,
        )

    loop(NR, lambda t: r_copy(t).start(), r)

    lane = lax.broadcasted_iota(jnp.int32, (O, 2 * O), 1)
    low = lane < O
    upper = jnp.where(low, 0, 1)
    sign = jnp.where(low, -1.0, 1.0).astype(jnp.float32)

    ret_load.wait()
    mir_load.wait()

    @pl.when(act)
    def _():
        def energy(t, carry):
            room = r * TR + t - c * TC
            for s2 in range(TC // 2):
                a0 = ret[t, 2 * s2].astype(jnp.float32)
                a1 = ret[t, 2 * s2 + 1].astype(jnp.float32)
                ar = jnp.where(low, a0, pltpu.roll(a1, O, 1))
                ai = jnp.where(low, pltpu.roll(a0, O, 1), a1)
                m = jnp.concatenate([mir[2 * s2, t], mir[2 * s2 + 1, t]], axis=0)
                mt = m.astype(jnp.float32).T
                mr, mi = mt[:O], mt[O:]
                sr = ar * ar - ai * ai
                si = 2.0 * ar * ai
                keep = upper + 2 * s2 <= room
                e_re = jnp.where(keep, sr * mr - si * mi, 0.0)
                e_im = jnp.where(keep, sr * mi + si * mr, 0.0)
                E[t, 0, :, s2 * 2 * O:(s2 + 1) * 2 * O] = e_re.astype(jnp.bfloat16)
                E[t, 1, :, s2 * 2 * O:(s2 + 1) * 2 * O] = e_im.astype(jnp.bfloat16)
            return carry

        lax.fori_loop(0, TR, energy, 0)

    init[...] = jnp.swapaxes(initial[...], 0, 1)
    cos, sin = jnp.cos(phase[...]), jnp.sin(phase[...])
    pow_re, pow_im = cos, sin
    for t in range(1, TR):
        pow_re, pow_im = pow_re * cos - pow_im * sin, pow_re * sin + pow_im * cos

    def spread(row):
        wide = jnp.concatenate([row, row], axis=1)
        return jnp.broadcast_to(wide, (2 * O, 2 * O)).T[:O]

    cos_k, sin_k = spread(cos), spread(sin) * sign
    pow_re_k, pow_im_k = spread(pow_re), spread(pow_im) * sign
    for t in range(TR):
        step = spread(retention[t:t + 1])
        fre[t] = step * cos_k
        fim[t] = step * sin_k

    def r_arrive(s):
        @pl.when(s != r)
        def _():
            pltpu.make_async_remote_copy(
                src_ref=rprod, dst_ref=rp.at[s],
                send_sem=rs.at[0], recv_sem=rr.at[s],
                device_id=(partner, c), device_id_type=MESH,
            ).wait_recv()

        @pl.when(s == r)
        def _():
            rp[s] = rprod[...]

        block = jnp.broadcast_to(rp[s, 0:1, :], (2 * O, 2 * O)).T[:O]
        kre[s] = block * pow_re_k
        kim[s] = block * pow_im_k

    loop(NR, r_arrive)

    second_hop(0)

    def z_up(q, p, src):
        return pltpu.make_async_remote_copy(
            src_ref=src.at[q, p], dst_ref=zl.at[q, p],
            send_sem=zsend.at[q, p], recv_sem=zrecv_l.at[q, p],
            device_id=(r, c + 1), device_id_type=MESH,
        )

    def z_down(q, p, src):
        return pltpu.make_async_remote_copy(
            src_ref=src.at[q, p], dst_ref=zr.at[q, p],
            send_sem=zsend.at[q, p], recv_sem=zrecv_r.at[q, p],
            device_id=(r, c - 1), device_id_type=MESH,
        )

    mine = pl.ds(pl.multiple_of(half * (O // 2), O // 2), O // 2)

    def pair_copy(p):
        return pltpu.make_async_remote_copy(
            src_ref=end_out.at[p], dst_ref=pair_end.at[p],
            send_sem=ps.at[p], recv_sem=pr.at[p],
            device_id=(partner, c), device_id_type=MESH,
        )

    def end_copy(p, target):
        return pltpu.make_async_remote_copy(
            src_ref=chip_end.at[p], dst_ref=ends.at[k, p, mine],
            send_sem=es.at[p, target], recv_sem=er.at[p, k, half],
            device_id=(target, c), device_id_type=MESH,
        )

    def later(fn):
        def body(t, carry):
            fn(t)
            return carry

        lax.fori_loop(2 * k + 2, NR, body, 0)

    def join_pair(p):
        pair_copy(p).wait_recv()
        theirs, own = pair_end[p, mine], end_out[p, mine]
        first = jnp.where(half == 0, own, theirs)
        second = jnp.where(half == 0, theirs, own)
        chip_end[p] = (
            kre[2 * k + 1, mine] * first + kim[2 * k + 1, mine] * pltpu.roll(first, O, 1) + second
        )
        later(lambda target: end_copy(p, target).start())

    def combine(h):
        for t in range(TR):
            a = acc[t, 0, :, h * 2 * O:(h + 1) * 2 * O]
            b = acc[t, 1, :, h * 2 * O:(h + 1) * 2 * O]
            tmp[h, t] = (a + sign * pltpu.roll(b, O, 1)) * norm

    def one_share(i, carry):
        q = share(i)
        up = goes_up(i)
        down = jnp.logical_and(i < NC - 1, jnp.logical_not(up))

        @pl.when(i + 2 < NC)
        def _():
            first_hop(i + 2)

        @pl.when(i + 1 < NC)
        def _():
            second_hop(i + 1)

        last_hop(i)

        def one_pair(pp, carry):
            @pl.when(act)
            def _():
                depth = TC * O
                rhs = jnp.concatenate(
                    [L[q, 2 * pp].reshape(depth, 2 * O), L[q, 2 * pp + 1].reshape(depth, 2 * O)],
                    axis=1,
                )
                lhs = E[...].reshape(TR * 2 * O, depth)
                acc[...] = jnp.dot(lhs, rhs, preferred_element_type=jnp.float32).reshape(
                    TR, 2, O, 4 * O
                )

            for h in range(2):
                p = 2 * pp + h

                @pl.when(act)
                def _():
                    combine(h)

                @pl.when(jnp.logical_and(up, has_left))
                def _():
                    z_up(q, p, zs).wait_recv()

                    @pl.when(act)
                    def _():
                        tmp[h] += zl[q, p].astype(jnp.float32)

                @pl.when(jnp.logical_and(up, act))
                def _():
                    zs[q, p] = tmp[h].astype(jnp.bfloat16)
                    z_up(q, p, zs).start()

                @pl.when(jnp.logical_and(up, jnp.logical_not(act)))
                def _():
                    z_up(q, p, zl).start()

                @pl.when(jnp.logical_and(down, act))
                def _():
                    @pl.when(act_right)
                    def _():
                        z_down(q, p, zs).wait_recv()
                        tmp[h] += zr[q, p].astype(jnp.float32)

                    zs[q, p] = tmp[h].astype(jnp.bfloat16)
                    z_down(q, p, zs).start()

                @pl.when(i == NC - 1)
                def _():
                    @pl.when(jnp.logical_not(act))
                    def _():
                        tmp[h] = jnp.zeros_like(tmp[h])

                    @pl.when(has_left)
                    def _():
                        z_up(q, p, zs).wait_recv()
                        tmp[h] += zl[q, p].astype(jnp.float32)

                    @pl.when(act_right)
                    def _():
                        z_down(q, p, zs).wait_recv()
                        tmp[h] += zr[q, p].astype(jnp.float32)

                    x = jnp.zeros((O, 2 * O), jnp.float32)
                    for t in range(TR):
                        v = tmp[h, t]
                        out[p, t] = v
                        x = x + v
                        x = fre[t] * x + fim[t] * pltpu.roll(x, O, 1)
                    end_out[p] = x
                    pair_copy(p).start()
                    join_pair(p)

            return carry

        return lax.fori_loop(0, PS // 2, one_pair, carry)

    lax.fori_loop(0, NC, one_share, 0)

    loop(NR, lambda t: r_copy(t).wait_send(), r)

    def drain_share(i, carry):
        q = share(i)
        up = goes_up(i)
        down = jnp.logical_and(i < NC - 1, jnp.logical_not(up))
        loop(n1, lambda n: l_first(i, n).wait_send(), m1)
        loop(n1, lambda s1: loop(n2, lambda n: l_second(i, s1, n).wait_send(), m2))

        @pl.when(act)
        def _():
            loop(pairs, lambda j: l_forward(i, j).wait_send())

        def z_one(p, carry):
            @pl.when(up)
            def _():
                z_up(q, p, zs).wait_send()

            @pl.when(jnp.logical_and(down, act))
            def _():
                z_down(q, p, zs).wait_send()

            return carry

        lax.fori_loop(0, PS, z_one, 0)
        return carry

    lax.fori_loop(0, NC, drain_share, 0)

    def enter(s, x):
        for p in range(PS):
            for h in range(2):
                part = pl.ds(h * (O // 2), O // 2)
                pltpu.make_async_remote_copy(
                    src_ref=chip_end.at[p], dst_ref=ends.at[s, p, part],
                    send_sem=es.at[p, 0], recv_sem=er.at[p, s, h],
                    device_id=(partner, c), device_id_type=MESH,
                ).wait_recv()
        for row in (2 * s, 2 * s + 1):
            x = kre[row] * x + kim[row] * pltpu.roll(x, O, 2)
        return x + ends[s]

    x = lax.fori_loop(0, k, enter, init[...])
    second = kre[2 * k] * x + kim[2 * k] * pltpu.roll(x, O, 2) + pair_end[...]
    x = jnp.where(half == 0, x, second)
    for t in range(TR):
        x = x + out[:, t]
        x = fre[t] * x + fim[t] * pltpu.roll(x, O, 2)
        out[:, t] = x

    def drain_end(p, carry):
        pair_copy(p).wait_send()
        later(lambda t: end_copy(p, t).wait_send())
        return carry

    lax.fori_loop(0, PS, drain_end, 0)


def per_device(retarded, mirrored, lesser_panel, initial, retention, phase_angle):
    NR = lax.axis_size("row")
    NC = lax.axis_size("col")
    TR, TC, O = retarded.shape[0], retarded.shape[1], retarded.shape[2]
    S2, PN = lesser_panel.shape[0], lesser_panel.shape[2]
    PS = PN // NC
    SK = S2 * O
    norm = 1.0 / (O * math.sqrt(TR * NR))
    XS = math.isqrt(NR // 2)
    while NR // 2 % XS:
        XS -= 1
    side = NR // 2 // XS
    f32, bf16 = jnp.float32, jnp.bfloat16
    dma = pltpu.SemaphoreType.DMA
    states = pl.pallas_call(
        functools.partial(kernel, NR, NC, TR, TC, O, PS, XS, norm),
        out_shape=jax.ShapeDtypeStruct((PS, TR, O, 2 * O), f32),
        in_specs=[pl.BlockSpec(memory_space=pl.ANY)] * 2
        + [pl.BlockSpec(memory_space=pltpu.VMEM)] * 4,
        out_specs=pl.BlockSpec(memory_space=pltpu.VMEM),
        scratch_shapes=[
            pltpu.VMEM(retarded.shape, bf16),
            pltpu.VMEM(mirrored.shape, bf16),
            pltpu.VMEM((PS, O, 2 * O), f32),
            pltpu.VMEM((TR, O, 2 * O), f32),
            pltpu.VMEM((TR, O, 2 * O), f32),
            pltpu.VMEM((8, 2 * O), f32),
            pltpu.VMEM((NR, O, 2 * O), f32),
            pltpu.VMEM((NR, O, 2 * O), f32),
            dma((2,)),
            pltpu.VMEM((TR, 2, O, TC * O), bf16),
            pltpu.VMEM((NC, PS, NR, SK, 2 * O), bf16),
            pltpu.VMEM((TR, 2, O, 4 * O), f32),
            pltpu.VMEM((2, TR, O, 2 * O), f32),
            pltpu.VMEM((NC, PS, TR, O, 2 * O), bf16),
            pltpu.VMEM((NC, PS, TR, O, 2 * O), bf16),
            pltpu.VMEM((NC, PS, TR, O, 2 * O), bf16),
            pltpu.VMEM((NR // 2, PS, O, 2 * O), f32),
            pltpu.VMEM((PS, O, 2 * O), f32),
            pltpu.VMEM((PS, O, 2 * O), f32),
            pltpu.VMEM((PS, O // 2, 2 * O), f32),
            pltpu.VMEM((NR, 8, 2 * O), f32),
            dma((NC, side)),
            dma((NC, side, side)),
            dma((NC, NR // 2)),
            dma((NC, NR)),
            dma((NC, PS)),
            dma((NC, PS)),
            dma((NC, PS)),
            dma((PS, NR)),
            dma((PS, NR // 2, 2)),
            dma((PS,)),
            dma((PS,)),
            dma((NR,)),
            dma((NR,)),
        ],
        compiler_params=pltpu.CompilerParams(
            collective_id=0, has_side_effects=True, vmem_limit_bytes=56 * 1024 * 1024
        ),
    )(retarded, mirrored, lesser_panel, initial, retention, phase_angle[None])
    return jnp.transpose(states, (1, 2, 0, 3))


def solution(mesh):
    return jax.shard_map(
        per_device,
        mesh=mesh,
        in_specs=(
            P("row", "col", None, None),
            P("col", "row", None, None),
            P(("col", "row"), None, None, None),
            P(None, "col", None),
            P("row", None),
            P(),
        ),
        out_specs=P("row", None, "col", None),
        check_vma=False,
    )
```

```python
import functools
import math

import jax
import jax.numpy as jnp
from jax import lax
from jax.experimental import pallas as pl
from jax.experimental.pallas import tpu as pltpu
from jax.sharding import PartitionSpec as P

MESH = pl.DeviceIdType.MESH


def kernel(
    NR, NC, TR, TC, O, PS, XS, norm,
    ret_in, mir_in, panel, initial, retention, phase,
    out,
    ret, mir, init, fre, fim, rprod, kre, kim, local_sem,
    E, L, acc, tmp, zl, zr, zs, ends, end_out, pair_end, chip_end, rp,
    l1, l2, lf, lr, zsend, zrecv_l, zrecv_r, es, er, ps, pr, rs, rr,
):
    r = lax.axis_index("row")
    c = lax.axis_index("col")
    half = lax.rem(r, 2)
    k = r // 2
    pairs = NR // 2
    YS = pairs // XS
    partner = r + 1 - 2 * half
    last_time = (k + 1) * 2 * TR - 1
    act = c * TC <= last_time
    act_right = jnp.logical_and(c + 1 < NC, (c + 1) * TC <= last_time)
    has_left = c > 0
    n_up = NC - 1 - c

    ret_load = pltpu.make_async_copy(ret_in, ret, local_sem.at[0])
    mir_load = pltpu.make_async_copy(mir_in, mir, local_sem.at[1])
    ret_load.start()
    mir_load.start()

    bar = pltpu.get_barrier_semaphore()

    def greet(j, carry):
        pl.semaphore_signal(bar, inc=1, device_id=(lax.rem(r + j, NR), c), device_id_type=MESH)
        return carry

    lax.fori_loop(1, NR, greet, 0)

    @pl.when(has_left)
    def _():
        pl.semaphore_signal(bar, inc=1, device_id=(r, c - 1), device_id_type=MESH)

    @pl.when(c < NC - 1)
    def _():
        pl.semaphore_signal(bar, inc=1, device_id=(r, c + 1), device_id_type=MESH)

    for s in range(panel.shape[0]):
        turned = jnp.swapaxes(panel[s].astype(jnp.float32), 0, 1).astype(jnp.bfloat16)
        for q in range(NC):
            L[q, :, r, s * O:(s + 1) * O] = turned[q * PS:(q + 1) * PS]
    kept = retention[0:1]
    for t in range(1, TR):
        kept = kept * retention[t:t + 1]
    rprod[...] = jnp.broadcast_to(jnp.concatenate([kept, kept], axis=1), rprod.shape)

    lane = lax.broadcasted_iota(jnp.int32, (O, 2 * O), 1)
    low = lane < O
    upper = jnp.where(low, 0, 1)
    sign = jnp.where(low, -1.0, 1.0).astype(jnp.float32)

    init[...] = jnp.swapaxes(initial[...], 0, 1)
    cos, sin = jnp.cos(phase[...]), jnp.sin(phase[...])
    pow_re, pow_im = cos, sin
    for t in range(1, TR):
        pow_re, pow_im = pow_re * cos - pow_im * sin, pow_re * sin + pow_im * cos

    def spread(row):
        wide = jnp.concatenate([row, row], axis=1)
        return jnp.broadcast_to(wide, (2 * O, 2 * O)).T[:O]

    cos_k, sin_k = spread(cos), spread(sin) * sign
    pow_re_k, pow_im_k = spread(pow_re), spread(pow_im) * sign
    for t in range(TR):
        step = spread(retention[t:t + 1])
        fre[t] = step * cos_k
        fim[t] = step * sin_k

    pl.semaphore_wait(
        bar, NR - 1 + jnp.where(has_left, 1, 0) + jnp.where(c < NC - 1, 1, 0)
    )

    both = jnp.minimum(n_up, c)

    def goes_up(i):
        turn = jnp.where(i < 2 * both, lax.rem(i, 2) == 0, n_up > c)
        return jnp.logical_and(i < NC - 1, turn)

    def share(i):
        nth = jnp.where(i < 2 * both, i // 2, i - both)
        return jnp.where(i < NC - 1, jnp.where(goes_up(i), NC - 1 - nth, nth), c)

    n1 = jnp.where(half == 0, XS, YS)
    n2 = jnp.where(half == 0, YS, XS)
    m1 = jnp.where(half == 0, lax.rem(k, XS), k // XS)
    m2 = jnp.where(half == 0, k // XS, lax.rem(k, XS))

    def chip(a1, a2):
        return jnp.where(half == 0, a2 * XS + a1, a1 * XS + a2)

    def panel_copy(i, source, target, send_sem):
        q = share(i)
        return pltpu.make_async_remote_copy(
            src_ref=L.at[q, :, source], dst_ref=L.at[q, :, source],
            send_sem=send_sem, recv_sem=lr.at[i, source],
            device_id=(target, c), device_id_type=MESH,
        )

    def l_first(i, n):
        return panel_copy(i, r, 2 * chip(n, m2) + half, l1.at[i, n])

    def l_second(i, s1, n):
        return panel_copy(i, 2 * chip(s1, m2) + half, 2 * chip(m1, n) + half, l2.at[i, s1, n])

    def l_forward(i, j):
        return panel_copy(i, 2 * j + half, partner, lf.at[i, j])

    def l_arrived(i, source):
        return panel_copy(i, source, partner, lf.at[i, 0])

    def loop(count, fn, skip=None):
        def body(n, carry):
            if skip is None:
                fn(n)
            else:
                @pl.when(n != skip)
                def _():
                    fn(n)
            return carry

        lax.fori_loop(0, count, body, 0)

    def first_hop(i):
        loop(n1, lambda n: l_first(i, n).start(), m1)

        @pl.when(act)
        def _():
            l_forward(i, k).start()

    def second_hop(i):
        loop(n2, lambda n: l_second(i, m1, n).start(), m2)

        def relay(s1):
            source = chip(s1, m2)
            l_arrived(i, 2 * source + half).wait_recv()
            loop(n2, lambda n: l_second(i, s1, n).start(), m2)

            @pl.when(act)
            def _():
                l_forward(i, source).start()

        loop(n1, relay, m1)

    def last_hop(i):
        def line(s2):
            def one(s1):
                source = chip(s1, s2)
                l_arrived(i, 2 * source + half).wait_recv()

                @pl.when(act)
                def _():
                    l_forward(i, source).start()

            loop(n1, one)

        loop(n2, line, m2)

        @pl.when(act)
        def _():
            loop(pairs, lambda j: l_arrived(i, 2 * j + 1 - half).wait_recv())

    for i in range(min(2, NC)):
        first_hop(i)

    def r_copy(target):
        return pltpu.make_async_remote_copy(
            src_ref=rprod, dst_ref=rp.at[r],
            send_sem=rs.at[target], recv_sem=rr.at[r],
            device_id=(target, c), device_id_type=MESH,
        )

    loop(NR, lambda t: r_copy(t).start(), r)

    ret_load.wait()
    mir_load.wait()

    @pl.when(act)
    def _():
        def energy(t, carry):
            room = r * TR + t - c * TC
            for s2 in range(TC // 2):
                a0 = ret[t, 2 * s2].astype(jnp.float32)
                a1 = ret[t, 2 * s2 + 1].astype(jnp.float32)
                ar = jnp.where(low, a0, pltpu.roll(a1, O, 1))
                ai = jnp.where(low, pltpu.roll(a0, O, 1), a1)
                m = jnp.concatenate([mir[2 * s2, t], mir[2 * s2 + 1, t]], axis=0)
                mt = m.astype(jnp.float32).T
                mr, mi = mt[:O], mt[O:]
                sr = ar * ar - ai * ai
                si = 2.0 * ar * ai
                keep = upper + 2 * s2 <= room
                e_re = jnp.where(keep, sr * mr - si * mi, 0.0)
                e_im = jnp.where(keep, sr * mi + si * mr, 0.0)
                E[t, 0, :, s2 * 2 * O:(s2 + 1) * 2 * O] = e_re.astype(jnp.bfloat16)
                E[t, 1, :, s2 * 2 * O:(s2 + 1) * 2 * O] = e_im.astype(jnp.bfloat16)
            return carry

        lax.fori_loop(0, TR, energy, 0)

    second_hop(0)

    def r_arrive(s):
        @pl.when(s != r)
        def _():
            pltpu.make_async_remote_copy(
                src_ref=rprod, dst_ref=rp.at[s],
                send_sem=rs.at[0], recv_sem=rr.at[s],
                device_id=(partner, c), device_id_type=MESH,
            ).wait_recv()

        @pl.when(s == r)
        def _():
            rp[s] = rprod[...]

        block = jnp.broadcast_to(rp[s, 0:1, :], (2 * O, 2 * O)).T[:O]
        kre[s] = block * pow_re_k
        kim[s] = block * pow_im_k

    def z_up(q, p, src):
        return pltpu.make_async_remote_copy(
            src_ref=src.at[q, p], dst_ref=zl.at[q, p],
            send_sem=zsend.at[q, p], recv_sem=zrecv_l.at[q, p],
            device_id=(r, c + 1), device_id_type=MESH,
        )

    def z_down(q, p, src):
        return pltpu.make_async_remote_copy(
            src_ref=src.at[q, p], dst_ref=zr.at[q, p],
            send_sem=zsend.at[q, p], recv_sem=zrecv_r.at[q, p],
            device_id=(r, c - 1), device_id_type=MESH,
        )

    mine = pl.ds(pl.multiple_of(half * (O // 2), O // 2), O // 2)

    def pair_copy(p):
        return pltpu.make_async_remote_copy(
            src_ref=end_out.at[p], dst_ref=pair_end.at[p],
            send_sem=ps.at[p], recv_sem=pr.at[p],
            device_id=(partner, c), device_id_type=MESH,
        )

    def end_copy(p, target):
        return pltpu.make_async_remote_copy(
            src_ref=chip_end.at[p], dst_ref=ends.at[k, p, mine],
            send_sem=es.at[p, target], recv_sem=er.at[p, k, half],
            device_id=(target, c), device_id_type=MESH,
        )

    def later(fn):
        def body(t, carry):
            fn(t)
            return carry

        lax.fori_loop(2 * k + 2, NR, body, 0)

    def join_pair(p):
        pair_copy(p).wait_recv()
        theirs, own = pair_end[p, mine], end_out[p, mine]
        first = jnp.where(half == 0, own, theirs)
        second = jnp.where(half == 0, theirs, own)
        chip_end[p] = (
            kre[2 * k + 1, mine] * first + kim[2 * k + 1, mine] * pltpu.roll(first, O, 1) + second
        )
        later(lambda target: end_copy(p, target).start())

    def combine(h):
        for t in range(TR):
            a = acc[t, 0, :, h * 2 * O:(h + 1) * 2 * O]
            b = acc[t, 1, :, h * 2 * O:(h + 1) * 2 * O]
            tmp[h, t] = (a + sign * pltpu.roll(b, O, 1)) * norm

    def one_share(i, carry):
        q = share(i)
        up = goes_up(i)
        down = jnp.logical_and(i < NC - 1, jnp.logical_not(up))

        @pl.when(i + 2 < NC)
        def _():
            first_hop(i + 2)

        @pl.when(i + 1 < NC)
        def _():
            second_hop(i + 1)

        @pl.when(i == min(1, NC - 1))
        def _():
            loop(NR, r_arrive)

        last_hop(i)

        def one_pair(pp, carry):
            @pl.when(act)
            def _():
                depth = TC * O
                rhs = jnp.concatenate(
                    [L[q, 2 * pp].reshape(depth, 2 * O), L[q, 2 * pp + 1].reshape(depth, 2 * O)],
                    axis=1,
                )
                lhs = E[...].reshape(TR * 2 * O, depth)
                acc[...] = jnp.dot(lhs, rhs, preferred_element_type=jnp.float32).reshape(
                    TR, 2, O, 4 * O
                )

            for h in range(2):
                p = 2 * pp + h

                @pl.when(act)
                def _():
                    combine(h)

                @pl.when(jnp.logical_and(up, has_left))
                def _():
                    z_up(q, p, zs).wait_recv()

                    @pl.when(act)
                    def _():
                        tmp[h] += zl[q, p].astype(jnp.float32)

                @pl.when(jnp.logical_and(up, act))
                def _():
                    zs[q, p] = tmp[h].astype(jnp.bfloat16)
                    z_up(q, p, zs).start()

                @pl.when(jnp.logical_and(up, jnp.logical_not(act)))
                def _():
                    z_up(q, p, zl).start()

                @pl.when(jnp.logical_and(down, act))
                def _():
                    @pl.when(act_right)
                    def _():
                        z_down(q, p, zs).wait_recv()
                        tmp[h] += zr[q, p].astype(jnp.float32)

                    zs[q, p] = tmp[h].astype(jnp.bfloat16)
                    z_down(q, p, zs).start()

                @pl.when(i == NC - 1)
                def _():
                    @pl.when(jnp.logical_not(act))
                    def _():
                        tmp[h] = jnp.zeros_like(tmp[h])

                    @pl.when(has_left)
                    def _():
                        z_up(q, p, zs).wait_recv()
                        tmp[h] += zl[q, p].astype(jnp.float32)

                    @pl.when(act_right)
                    def _():
                        z_down(q, p, zs).wait_recv()
                        tmp[h] += zr[q, p].astype(jnp.float32)

                    x = jnp.zeros((O, 2 * O), jnp.float32)
                    for t in range(TR):
                        v = tmp[h, t]
                        out[p, t] = v
                        x = x + v
                        x = fre[t] * x + fim[t] * pltpu.roll(x, O, 1)
                    end_out[p] = x
                    pair_copy(p).start()
                    join_pair(p)

            return carry

        return lax.fori_loop(0, PS // 2, one_pair, carry)

    lax.fori_loop(0, NC, one_share, 0)

    loop(NR, lambda t: r_copy(t).wait_send(), r)

    def drain_share(i, carry):
        q = share(i)
        up = goes_up(i)
        down = jnp.logical_and(i < NC - 1, jnp.logical_not(up))
        loop(n1, lambda n: l_first(i, n).wait_send(), m1)
        loop(n1, lambda s1: loop(n2, lambda n: l_second(i, s1, n).wait_send(), m2))

        @pl.when(act)
        def _():
            loop(pairs, lambda j: l_forward(i, j).wait_send())

        def z_one(p, carry):
            @pl.when(up)
            def _():
                z_up(q, p, zs).wait_send()

            @pl.when(jnp.logical_and(down, act))
            def _():
                z_down(q, p, zs).wait_send()

            return carry

        lax.fori_loop(0, PS, z_one, 0)
        return carry

    lax.fori_loop(0, NC, drain_share, 0)

    def enter(s, x):
        for p in range(PS):
            for h in range(2):
                part = pl.ds(h * (O // 2), O // 2)
                pltpu.make_async_remote_copy(
                    src_ref=chip_end.at[p], dst_ref=ends.at[s, p, part],
                    send_sem=es.at[p, 0], recv_sem=er.at[p, s, h],
                    device_id=(partner, c), device_id_type=MESH,
                ).wait_recv()
        for row in (2 * s, 2 * s + 1):
            x = kre[row] * x + kim[row] * pltpu.roll(x, O, 2)
        return x + ends[s]

    x = lax.fori_loop(0, k, enter, init[...])
    second = kre[2 * k] * x + kim[2 * k] * pltpu.roll(x, O, 2) + pair_end[...]
    x = jnp.where(half == 0, x, second)
    for t in range(TR):
        x = x + out[:, t]
        x = fre[t] * x + fim[t] * pltpu.roll(x, O, 2)
        out[:, t] = x

    def drain_end(p, carry):
        pair_copy(p).wait_send()
        later(lambda t: end_copy(p, t).wait_send())
        return carry

    lax.fori_loop(0, PS, drain_end, 0)


def per_device(retarded, mirrored, lesser_panel, initial, retention, phase_angle):
    NR = lax.axis_size("row")
    NC = lax.axis_size("col")
    TR, TC, O = retarded.shape[0], retarded.shape[1], retarded.shape[2]
    S2, PN = lesser_panel.shape[0], lesser_panel.shape[2]
    PS = PN // NC
    SK = S2 * O
    norm = 1.0 / (O * math.sqrt(TR * NR))
    XS = math.isqrt(NR // 2)
    while NR // 2 % XS:
        XS -= 1
    side = NR // 2 // XS
    f32, bf16 = jnp.float32, jnp.bfloat16
    dma = pltpu.SemaphoreType.DMA
    states = pl.pallas_call(
        functools.partial(kernel, NR, NC, TR, TC, O, PS, XS, norm),
        out_shape=jax.ShapeDtypeStruct((PS, TR, O, 2 * O), f32),
        in_specs=[pl.BlockSpec(memory_space=pl.ANY)] * 2
        + [pl.BlockSpec(memory_space=pltpu.VMEM)] * 4,
        out_specs=pl.BlockSpec(memory_space=pltpu.VMEM),
        scratch_shapes=[
            pltpu.VMEM(retarded.shape, bf16),
            pltpu.VMEM(mirrored.shape, bf16),
            pltpu.VMEM((PS, O, 2 * O), f32),
            pltpu.VMEM((TR, O, 2 * O), f32),
            pltpu.VMEM((TR, O, 2 * O), f32),
            pltpu.VMEM((8, 2 * O), f32),
            pltpu.VMEM((NR, O, 2 * O), f32),
            pltpu.VMEM((NR, O, 2 * O), f32),
            dma((2,)),
            pltpu.VMEM((TR, 2, O, TC * O), bf16),
            pltpu.VMEM((NC, PS, NR, SK, 2 * O), bf16),
            pltpu.VMEM((TR, 2, O, 4 * O), f32),
            pltpu.VMEM((2, TR, O, 2 * O), f32),
            pltpu.VMEM((NC, PS, TR, O, 2 * O), bf16),
            pltpu.VMEM((NC, PS, TR, O, 2 * O), bf16),
            pltpu.VMEM((NC, PS, TR, O, 2 * O), bf16),
            pltpu.VMEM((NR // 2, PS, O, 2 * O), f32),
            pltpu.VMEM((PS, O, 2 * O), f32),
            pltpu.VMEM((PS, O, 2 * O), f32),
            pltpu.VMEM((PS, O // 2, 2 * O), f32),
            pltpu.VMEM((NR, 8, 2 * O), f32),
            dma((NC, side)),
            dma((NC, side, side)),
            dma((NC, NR // 2)),
            dma((NC, NR)),
            dma((NC, PS)),
            dma((NC, PS)),
            dma((NC, PS)),
            dma((PS, NR)),
            dma((PS, NR // 2, 2)),
            dma((PS,)),
            dma((PS,)),
            dma((NR,)),
            dma((NR,)),
        ],
        compiler_params=pltpu.CompilerParams(
            collective_id=0, has_side_effects=True, vmem_limit_bytes=56 * 1024 * 1024
        ),
    )(retarded, mirrored, lesser_panel, initial, retention, phase_angle[None])
    return jnp.transpose(states, (1, 2, 0, 3))


def solution(mesh):
    return jax.shard_map(
        per_device,
        mesh=mesh,
        in_specs=(
            P("row", "col", None, None),
            P("col", "row", None, None),
            P(("col", "row"), None, None, None),
            P(None, "col", None),
            P("row", None),
            P(),
        ),
        out_specs=P("row", None, "col", None),
        check_vma=False,
    )
```
